32 devices in a mesh: frame: 4 (over z), dom: 2 (over x), coef: 4 (over y, core).
Axes of the slice: x: 2, y: 2, z: 4, core: 2. Of those that a mesh axis runs over, the one named last changes fastest.
Arguments:
- geometry: float32 [32, 32768], P('coef', ('frame', 'dom')), may hold values from -1 to 1
- fraction: float32 [32, 32768], P('coef', ('frame', 'dom')), may hold values from 0 to 1
- interval: int32 [32, 32768], P('coef', ('frame', 'dom')), may hold values from 0 to 156
- pattern: int32 [32, 256], P('coef', ('frame', 'dom')), may hold values from 0 to 95
- target: float32 [32768], P(('frame', 'dom')), may hold values from -8 to 8
Outputs:
- solution: float32 [384, 160], P('coef')
- residual: float32 [32768], P(('frame', 'dom'))
The draws below stay inside these ranges and needn't reach their ends.
Inputs may be any that keep to these rules, and one draw needn't show every extreme that they name: The spline of a slot reads coefficients interval to interval + 3 of its type. Slot s refers to pair type (s // 8) * 96 + pattern.
All inputs are finite; a program needn't handle non-finite values.
Results may differ from the reference program's by a relative error of at most 0.0003.
Values sent between devices are 32-bit elements; how exact they have to be, the bound alone decides.
A program may use at most 64 MiB of HBM per device.

```python
import jax
import jax.numpy as jnp
from jax import lax

NK = 160
TYPES = 384
NB = 8
ITERS = 2
ROWS = 32768
SLOTS = 32
TILES = 256
TYPES_DEV = 96
N_COEF = 4


def place_ends(values, own_key, low, largest):
    index_at = [jax.random.randint(jax.random.fold_in(own_key, axis), (), 0, length) for axis, length in enumerate(values.shape)]
    widest = values.shape.index(max(values.shape))
    next_to = index_at[:widest] + [(index_at[widest] + 1) % values.shape[widest]] + index_at[widest + 1:]
    return values.at[tuple(index_at)].set(low).at[tuple(next_to)].set(largest)


def level_of(stream_key, shape, shards, low, high):
    gain = 1.0
    for axis_at, parts in shards:
        draws = jax.random.uniform(jax.random.fold_in(jax.random.fold_in(stream_key, 6), axis_at), (parts,), jnp.float32, low / len(shards), high / len(shards))
        gain = gain * jnp.repeat(jnp.exp(draws), shape[axis_at] // parts).reshape((-1,) + (1,) * (len(shape) - 1 - axis_at))
    return gain


def scatter_about(own_key, dims, spread, most, cuts=(), kind=jnp.bfloat16):
    result = spread * jax.random.normal(own_key, dims, jnp.float32)
    if cuts:
        result = result * level_of(own_key, dims, cuts, -0.22, 0.18)
    return jnp.clip(result, -most, most).astype(kind)


def setup_inputs(seed: int = 0) -> dict:
    streams_of = jax.random.split(jax.random.key(seed), 6)
    geometry = jnp.clip(jax.random.uniform(streams_of[0], (SLOTS, ROWS), jnp.float32, -1.0, 1.0) * level_of(streams_of[0], (SLOTS, ROWS), ((0, 4), (1, 8)), -0.4, 0.0), -1.0, 1.0)
    fraction = jnp.clip(1.0 * jax.random.uniform(streams_of[1], (SLOTS, ROWS), jnp.float32) ** level_of(streams_of[1], (SLOTS, ROWS), ((0, 4), (1, 8)), -0.2, 0.2), 0.0, 1.0)
    interval = place_ends(jax.random.randint(streams_of[2], (SLOTS, ROWS), 0, NK - 3), jax.random.fold_in(streams_of[2], 1), 0, (NK - 3) - 1).astype(jnp.int32)
    pattern = place_ends(jax.random.randint(streams_of[3], (SLOTS, TILES), 0, TYPES_DEV), jax.random.fold_in(streams_of[3], 1), 0, TYPES_DEV - 1).astype(jnp.int32)
    target = scatter_about(streams_of[4], (ROWS,), 1.0, 8.0, ((0, 8),), jnp.float32)
    return dict(geometry=geometry, fraction=fraction, interval=interval, pattern=pattern, target=target)


def spline_weights(fraction):
    square = fraction * fraction
    cube = square * fraction
    return ((1.0 - fraction) ** 3 / 6.0, (3.0 * cube - 6.0 * square + 4.0) / 6.0,
            (-3.0 * cube + 3.0 * square + 3.0 * fraction + 1.0) / 6.0, cube / 6.0)


def reference(geometry, fraction, interval, pattern, target):
    per_coef = TYPES // N_COEF
    slot_ids = jnp.arange(SLOTS, dtype=jnp.int32)
    kinds = ((slot_ids // NB) * per_coef).astype(jnp.int32)[:, None] + pattern

    def slot_data(slot):
        row_kind = jnp.repeat(kinds[slot], 128)
        base = (row_kind * NK + interval[slot]).astype(jnp.int32)
        weights = spline_weights(fraction[slot])
        return base, weights, geometry[slot]

    def forward(flat):
        def step(image, slot):
            base, weights, geom = slot_data(slot)
            value = jnp.zeros((ROWS,), jnp.float32)
            for offset in range(4):
                value = value + weights[offset] * flat[base + offset]
            return image + geom * value, None
        image, _ = lax.scan(step, jnp.zeros((ROWS,), jnp.float32), slot_ids)
        return image

    def backward(resid):
        def step(total, slot):
            base, weights, geom = slot_data(slot)
            for offset in range(4):
                total = total.at[base + offset].add(geom * weights[offset] * resid)
            return total, None
        total, _ = lax.scan(step, jnp.zeros((TYPES * NK,), jnp.float32), slot_ids)
        return total

    residual = target
    gradient = backward(residual)
    gamma = jnp.sum(gradient * gradient)
    direction = gradient
    solution = jnp.zeros_like(gradient)
    for step_index in range(ITERS):
        image = forward(direction)
        alpha = gamma / jnp.sum(image * image)
        solution = solution + alpha * direction
        residual = residual - alpha * image
        if step_index + 1 < ITERS:
            gradient = backward(residual)
            gamma_next = jnp.sum(gradient * gradient)
            direction = gradient + (gamma_next / gamma) * direction
            gamma = gamma_next
    return solution.reshape(TYPES, NK), residual
```

```python
import functools

import jax
import jax.numpy as jnp
from jax import lax
from jax.experimental import pallas as pl
from jax.experimental.pallas import tpu as pltpu
from jax.sharding import PartitionSpec as P

NK = 160
TYPES = 384
LANES = 128
LOW = 16
HIGHS = NK // LOW
SPREAD = LOW + 4
MESH = pl.DeviceIdType.MESH
F32 = jnp.float32
BF16 = jnp.bfloat16


def iota(shape, axis):
    return lax.broadcasted_iota(jnp.int32, shape, axis)


def split(x):
    top = x.astype(BF16)
    return top, (x - top.astype(F32)).astype(BF16)


def total_of(x):
    return jnp.sum(jnp.sum(x, axis=0, keepdims=True), axis=1, keepdims=True)


def each(count, body):
    if count <= 8:
        for index in range(count):
            body(index)
    else:
        lax.fori_loop(0, count, lambda index, _: (body(index), 0)[1], 0)


def kernel(n, nd, nc, share, geom_ref, frac_ref, knot_ref, patt_ref, targ_ref, sol_ref, res_ref,
           gw, z, table, picks, picks_t, fold, send_buf, rs_buf, ag_buf, im_buf, fin_buf,
           rs_send, rs_recv, ag_send, ag_recv, im_send, im_recv, fin_send, fin_recv):
    nb, rows = geom_ref.shape
    tiles = rows // LANES
    pairs = tiles * nb
    per_coef = TYPES // nc
    wide = picks.shape[1] // 2
    quarter = per_coef // 4
    at_dom = lax.axis_index("dom")
    at_coef = lax.axis_index("coef")
    at_frame = lax.axis_index("frame")
    me = at_frame * nd + at_dom

    def member(step):
        return lax.rem(me + step, n)

    def member_id(p):
        return (lax.div(p, nd), lax.rem(p, nd), at_coef)

    def coef_peer(step):
        return lax.rem(at_coef + step, nc)

    def coef_id(p):
        return (at_frame, at_dom, p)

    barrier = pltpu.get_barrier_semaphore()
    each(n - 1, lambda k: pl.semaphore_signal(barrier, inc=1, device_id=member_id(member(k + 1)), device_id_type=MESH))
    each(nc - 1, lambda k: pl.semaphore_signal(barrier, inc=1, device_id=coef_id(coef_peer(k + 1)), device_id_type=MESH))

    kinds = patt_ref[...].astype(F32).astype(BF16)
    spread = (iota((tiles, pairs), 1) >= nb * iota((tiles, pairs), 0)) & (iota((tiles, pairs), 1) < nb * (iota((tiles, pairs), 0) + 1))
    across = jnp.dot(kinds, jnp.where(spread, 1.0, 0.0).astype(BF16), preferred_element_type=F32)
    own = (iota((nb, pairs), 1) & (nb - 1)) == iota((nb, pairs), 0)
    across = jnp.sum(jnp.where(own, across, 0.0), axis=0, keepdims=True).astype(jnp.int32)
    hot_t = jnp.where(across == iota((per_coef, pairs), 0), 1.0, 0.0).astype(BF16)
    picks_t[...] = jnp.concatenate([hot_t, hot_t], axis=1)
    spread = (iota((pairs, tiles), 0) >= nb * iota((pairs, tiles), 1)) & (iota((pairs, tiles), 0) < nb * (iota((pairs, tiles), 1) + 1))
    down = lax.dot_general(jnp.where(spread, 1.0, 0.0).astype(BF16), kinds, (((1,), (1,)), ((), ())), preferred_element_type=F32)
    own = (iota((pairs, nb), 0) & (nb - 1)) == iota((pairs, nb), 1)
    down = jnp.sum(jnp.where(own, down, 0.0), axis=1, keepdims=True).astype(jnp.int32)
    hot = jnp.where(down == iota((pairs, wide), 1), 1.0, 0.0).astype(BF16)
    picks[...] = jnp.concatenate([hot, hot], axis=1)
    lows = iota((SPREAD * nb, 2 * LANES), 0) // nb
    for h in range(HIGHS):
        fold[h] = jnp.where(iota((SPREAD * nb, 2 * LANES), 1) == lows + LOW * h, 1.0, 0.0).astype(BF16)

    same_slot = (iota((HIGHS * nb, SPREAD * nb), 0) & (nb - 1)) == (iota((HIGHS * nb, SPREAD * nb), 1) & (nb - 1))

    def weigh(at):
        u = frac_ref[:, at]
        g = geom_ref[:, at] * (1.0 / 6.0)
        square = u * u
        cube = square * u
        less = 1.0 - u
        gw[0, :, at] = g * (less * less * less)
        gw[1, :, at] = g * (3.0 * cube - 6.0 * square + 4.0)
        gw[2, :, at] = g * (-3.0 * cube + 3.0 * square + 3.0 * u + 1.0)
        gw[3, :, at] = g * cube

    def backward(value_ref, first):
        def block(b, carry):
            values = value_ref[pl.ds(pl.multiple_of(8 * b, 8), 8), :]
            for k in range(8):
                at = pl.ds(pl.multiple_of((8 * b + k) * LANES, LANES), LANES)
                if first:
                    weigh(at)
                knot = knot_ref[:, at]
                high, low = knot >> 4, knot & (LOW - 1)
                value = values[k:k + 1, :]
                terms = [gw[j, :, at] * value for j in range(4)]
                hits = [low == m for m in range(LOW)]
                parts = []
                for m in range(SPREAD):
                    part = jnp.zeros((nb, LANES), F32)
                    for j in range(4):
                        if 0 <= m - j < LOW:
                            part = jnp.where(hits[m - j], terms[j], part)
                    parts.append(part)
                right = jnp.concatenate(split(jnp.concatenate(parts, axis=0)), axis=1)
                left = jnp.concatenate([jnp.where(high == h, 1.0, 0.0) for h in range(HIGHS)], axis=0).astype(BF16)
                left = jnp.concatenate([left, left], axis=1)
                prod = lax.dot_general(left, right, (((1,), (1,)), ((), ())), preferred_element_type=F32)
                prod = jnp.where(same_slot, prod, 0.0)
                for h in range(HIGHS):
                    z[h, pl.ds(pl.multiple_of((8 * b + k) * nb, nb), nb), :] = prod[h * nb:(h + 1) * nb, :]
            return carry

        lax.fori_loop(0, tiles // 8, block, 0)
        grad = jnp.zeros((per_coef, 2 * LANES), F32)
        for h in range(HIGHS):
            chosen = jnp.dot(picks_t[...], jnp.concatenate(split(z[h]), axis=0), preferred_element_type=F32)
            for piece in split(chosen):
                grad = grad + jnp.dot(piece, fold[h], preferred_element_type=F32)
        tail = grad[:quarter, LANES:]
        for q in range(1, 4):
            tail = tail + pltpu.roll(grad[q * quarter:(q + 1) * quarter, LANES:], 32 * q, 1)
        filled = per_coef + quarter
        return jnp.concatenate([grad[:, :LANES], tail, jnp.zeros((n * share - filled, LANES), F32)], axis=0)

    def tails(packed):
        tail = packed[per_coef:per_coef + quarter, :]
        return [tail] + [pltpu.roll(tail, LANES - 32 * q, 1) for q in range(1, 4)]

    def forward(packed, out):
        upper = jnp.concatenate(tails(packed) + [jnp.zeros((wide - per_coef, LANES), F32)], axis=0)
        lower = jnp.concatenate([packed[:per_coef, :], jnp.zeros((wide - per_coef, LANES), F32)], axis=0)
        coeffs = jnp.concatenate([lower, upper], axis=1)
        table[...] = jnp.dot(picks[...], jnp.concatenate(split(coeffs), axis=0), preferred_element_type=F32)

        def block(b, carry):
            sums = []
            for k in range(8):
                at = pl.ds(pl.multiple_of((8 * b + k) * LANES, LANES), LANES)
                span = pl.ds(pl.multiple_of((8 * b + k) * nb, nb), nb)
                below, above = table[span, :LANES], table[span, LANES:]
                knot = knot_ref[:, at]
                force = jnp.zeros((nb, LANES), F32)
                for j in range(4):
                    index = knot + j
                    lane = index & (LANES - 1)
                    found = jnp.where(
                        index < LANES,
                        jnp.take_along_axis(below, lane, axis=1, mode="promise_in_bounds"),
                        jnp.take_along_axis(above, lane, axis=1, mode="promise_in_bounds"),
                    )
                    force = force + gw[j, :, at] * found
                sums.append(jnp.sum(force, axis=0, keepdims=True))
            im_buf[out, at_coef, pl.ds(pl.multiple_of(8 * b, 8), 8), :] = jnp.concatenate(sums, axis=0)
            return carry

        lax.fori_loop(0, tiles // 8, block, 0)
        im_buf[out, at_coef, tiles:tiles + 8, :] = jnp.broadcast_to(total_of(packed * packed), (8, LANES))

    def copies(kind, phase, step):
        p = member(step) if kind != "im" else coef_peer(step)
        if kind == "rs":
            count = share + 8 * phase
            return (send_buf.at[phase, p, pl.ds(0, count)], rs_buf.at[phase, me, pl.ds(0, count)], rs_send.at[phase, p], rs_recv.at[phase, me], member_id(p))
        if kind == "ag":
            return (ag_buf.at[phase, me], ag_buf.at[phase, me], ag_send.at[phase, p], ag_recv.at[phase, me], member_id(p))
        if kind == "im":
            return (im_buf.at[phase, at_coef], im_buf.at[phase, at_coef], im_send.at[phase, p], im_recv.at[phase, at_coef], coef_id(p))
        return (fin_buf.at[me], fin_buf.at[me], fin_send.at[p], fin_recv.at[me], member_id(p))

    def landing(kind, phase, step):
        p = member(step) if kind != "im" else coef_peer(step)
        if kind == "rs":
            count = share + 8 * phase
            return (send_buf.at[phase, p, pl.ds(0, count)], rs_buf.at[phase, p, pl.ds(0, count)], rs_send.at[phase, p], rs_recv.at[phase, p], member_id(p))
        if kind == "ag":
            return (ag_buf.at[phase, p], ag_buf.at[phase, p], ag_send.at[phase, p], ag_recv.at[phase, p], member_id(p))
        if kind == "im":
            return (im_buf.at[phase, p], im_buf.at[phase, p], im_send.at[phase, p], im_recv.at[phase, p], coef_id(p))
        return (fin_buf.at[p], fin_buf.at[p], fin_send.at[p], fin_recv.at[p], member_id(p))

    def remote(parts):
        return pltpu.make_async_remote_copy(src_ref=parts[0], dst_ref=parts[1], send_sem=parts[2], recv_sem=parts[3], device_id=parts[4], device_id_type=MESH)

    def start(kind, phase, count):
        each(count - 1, lambda k: remote(copies(kind, phase, k + 1)).start())

    def arrive(kind, phase, count):
        each(count - 1, lambda k: remote(landing(kind, phase, k + 1)).wait_recv())

    def drain(kind, phase, count):
        each(count - 1, lambda k: remote(copies(kind, phase, k + 1)).wait_send())

    def scatter_sum(packed, phase, extra):
        for p in range(n):
            send_buf[phase, p, :share, :] = packed[p * share:(p + 1) * share, :]
            if extra is not None:
                send_buf[phase, p, share:share + 8, :] = jnp.broadcast_to(extra, (8, LANES))
        start("rs", phase, n)
        rs_buf[phase, me] = send_buf[phase, me]
        arrive("rs", phase, n)
        sums = rs_buf[phase, 0]
        for p in range(1, n):
            sums = sums + rs_buf[phase, p]
        return sums

    def gather(part, phase):
        ag_buf[phase, me] = part
        start("ag", phase, n)
        arrive("ag", phase, n)
        return ag_buf[phase].reshape(n * share, LANES)

    def exchange(phase):
        start("im", phase, nc)
        arrive("im", phase, nc)
        sums = im_buf[phase, 0]
        for p in range(1, nc):
            sums = sums + im_buf[phase, p]
        return sums[:tiles], sums[tiles:tiles + 1, :1]

    packed = backward(targ_ref, True)
    send_buf[...] = jnp.zeros(send_buf.shape, F32)
    pl.semaphore_wait(barrier, n - 1 + nc - 1)
    part = scatter_sum(packed, 0, None)[:share]
    grad = gather(part, 0)
    forward(grad, 0)
    image, gamma = exchange(0)
    res_ref[...] = image
    packed = backward(res_ref, False)
    sums = scatter_sum(packed, 1, total_of(image * image))
    alpha = gamma / sums[share:share + 1, :1]
    part = part - alpha * sums[:share]
    grad_next = gather(part, 1)
    forward(grad_next, 1)
    image_next, gamma_next = exchange(1)
    beta = gamma_next / gamma
    image_next = image_next + beta * image
    fin_buf[me] = jnp.broadcast_to(total_of(image_next * image_next), (8, LANES))
    start("fin", 0, n)
    direction = grad_next + beta * grad
    arrive("fin", 0, n)
    norm = fin_buf[0, :1, :1]
    for p in range(1, n):
        norm = norm + fin_buf[p, :1, :1]
    alpha_next = gamma_next / norm
    answer = alpha * grad + alpha_next * direction
    sol_ref[:, :LANES] = answer[:per_coef]
    for q, tail in enumerate(tails(answer)):
        sol_ref[q * quarter:(q + 1) * quarter, LANES:] = tail[:, :NK - LANES]
    res_ref[...] = targ_ref[...] - alpha * image - alpha_next * image_next
    for phase in range(2):
        drain("rs", phase, n)
        drain("ag", phase, n)
        drain("im", phase, nc)
    drain("fin", 0, n)


def on_device(n, nd, nc, geometry, fraction, interval, pattern, target):
    nb, rows = geometry.shape
    tiles = rows // LANES
    pairs = tiles * nb
    per_coef = TYPES // nc
    wide = -(-per_coef // LANES) * LANES
    share = -(-(per_coef + per_coef // 4) // (8 * n)) * 8
    sem = pltpu.SemaphoreType.DMA
    vmem = pl.BlockSpec(memory_space=pltpu.VMEM)
    solved, left = pl.pallas_call(
        functools.partial(kernel, n, nd, nc, share),
        out_shape=(jax.ShapeDtypeStruct((per_coef, NK), F32), jax.ShapeDtypeStruct((tiles, LANES), F32)),
        in_specs=[vmem] * 5,
        out_specs=(vmem, vmem),
        scratch_shapes=[
            pltpu.VMEM((4, nb, rows), F32),
            pltpu.VMEM((HIGHS, pairs, SPREAD * nb), F32),
            pltpu.VMEM((pairs, 2 * LANES), F32),
            pltpu.VMEM((pairs, 2 * wide), BF16),
            pltpu.VMEM((per_coef, 2 * pairs), BF16),
            pltpu.VMEM((HIGHS, SPREAD * nb, 2 * LANES), BF16),
            pltpu.VMEM((2, n, share + 8, LANES), F32),
            pltpu.VMEM((2, n, share + 8, LANES), F32),
            pltpu.VMEM((2, n, share, LANES), F32),
            pltpu.VMEM((2, nc, tiles + 8, LANES), F32),
            pltpu.VMEM((n, 8, LANES), F32),
            sem((2, n)), sem((2, n)), sem((2, n)), sem((2, n)), sem((2, nc)), sem((2, nc)), sem((n,)), sem((n,)),
        ],
        compiler_params=pltpu.CompilerParams(collective_id=0, has_side_effects=True, vmem_limit_bytes=40 * 1024 * 1024),
    )(geometry, fraction, interval, pattern, target.reshape(tiles, LANES))
    return solved, left.reshape(rows)


def solution(mesh):
    sizes = dict(mesh.shape)
    n, nd, nc = sizes["frame"] * sizes["dom"], sizes["dom"], sizes["coef"]
    both = P("coef", ("frame", "dom"))
    return jax.shard_map(
        functools.partial(on_device, n, nd, nc),
        mesh=mesh,
        in_specs=(both, both, both, both, P(("frame", "dom"))),
        out_specs=(P("coef", None), P(("frame", "dom"))),
        check_vma=False,
    )
```

```python
import functools

import jax
import jax.numpy as jnp
from jax import lax
from jax.experimental import pallas as pl
from jax.experimental.pallas import tpu as pltpu
from jax.sharding import PartitionSpec as P

NK = 160
TYPES = 384
LANES = 128
LOW = 16
HIGHS = NK // LOW
SPREAD = LOW + 4
MESH = pl.DeviceIdType.MESH
F32 = jnp.float32
BF16 = jnp.bfloat16


def iota(shape, axis):
    return lax.broadcasted_iota(jnp.int32, shape, axis)


def split(x):
    top = x.astype(BF16)
    return top, (x - top.astype(F32)).astype(BF16)


def total_of(x):
    return jnp.sum(jnp.sum(x, axis=0, keepdims=True), axis=1, keepdims=True)


def each(count, body):
    if count <= 8:
        for index in range(count):
            body(index)
    else:
        lax.fori_loop(0, count, lambda index, _: (body(index), 0)[1], 0)


def kernel(n, nd, nc, share, geom_hbm, frac_hbm, knot_hbm, patt_hbm, targ_hbm, sol_ref, res_ref,
           geom_ref, frac_ref, knot_ref, patt_ref, targ_ref, image_ref,
           gw, z, table, picks, picks_t, fold, send_buf, rs_buf, ag_buf, im_buf, gm_buf, nm_buf, load_sem,
           rs_send, rs_recv, ag_send, ag_recv, im_send, im_recv, gm_send, gm_recv, nm_send, nm_recv):
    loads = [
        pltpu.make_async_copy(src, dst, load_sem.at[k])
        for k, (src, dst) in enumerate(((patt_hbm, patt_ref), (frac_hbm, frac_ref), (geom_hbm, geom_ref), (knot_hbm, knot_ref), (targ_hbm, targ_ref)))
    ]
    for load in loads:
        load.start()
    nb, rows = geom_ref.shape
    tiles = rows // LANES
    pairs = tiles * nb
    per_coef = TYPES // nc
    wide = picks.shape[1] // 2
    quarter = per_coef // 4
    at_dom = lax.axis_index("dom")
    at_coef = lax.axis_index("coef")
    at_frame = lax.axis_index("frame")
    me = at_frame * nd + at_dom

    def member(step):
        return lax.rem(me + step, n)

    def member_id(p):
        return (lax.div(p, nd), lax.rem(p, nd), at_coef)

    def coef_peer(step):
        return lax.rem(at_coef + step, nc)

    def coef_id(p):
        return (at_frame, at_dom, p)

    barrier = pltpu.get_barrier_semaphore()
    each(n - 1, lambda k: pl.semaphore_signal(barrier, inc=1, device_id=member_id(member(k + 1)), device_id_type=MESH))
    each(nc - 1, lambda k: pl.semaphore_signal(barrier, inc=1, device_id=coef_id(coef_peer(k + 1)), device_id_type=MESH))

    lows = iota((SPREAD * nb, 2 * LANES), 0) // nb
    for h in range(HIGHS):
        fold[h] = jnp.where(iota((SPREAD * nb, 2 * LANES), 1) == lows + LOW * h, 1.0, 0.0).astype(BF16)
    same_slot = (iota((HIGHS * nb, SPREAD * nb), 0) & (nb - 1)) == (iota((HIGHS * nb, SPREAD * nb), 1) & (nb - 1))

    loads[0].wait()
    kinds = patt_ref[...].astype(F32).astype(BF16)
    spread = (iota((tiles, pairs), 1) >= nb * iota((tiles, pairs), 0)) & (iota((tiles, pairs), 1) < nb * (iota((tiles, pairs), 0) + 1))
    across = jnp.dot(kinds, jnp.where(spread, 1.0, 0.0).astype(BF16), preferred_element_type=F32)
    own = (iota((nb, pairs), 1) & (nb - 1)) == iota((nb, pairs), 0)
    across = jnp.sum(jnp.where(own, across, 0.0), axis=0, keepdims=True).astype(jnp.int32)
    hot_t = jnp.where(across == iota((per_coef, pairs), 0), 1.0, 0.0).astype(BF16)
    picks_t[...] = jnp.concatenate([hot_t, hot_t], axis=1)
    spread = (iota((pairs, tiles), 0) >= nb * iota((pairs, tiles), 1)) & (iota((pairs, tiles), 0) < nb * (iota((pairs, tiles), 1) + 1))
    down = lax.dot_general(jnp.where(spread, 1.0, 0.0).astype(BF16), kinds, (((1,), (1,)), ((), ())), preferred_element_type=F32)
    own = (iota((pairs, nb), 0) & (nb - 1)) == iota((pairs, nb), 1)
    down = jnp.sum(jnp.where(own, down, 0.0), axis=1, keepdims=True).astype(jnp.int32)
    hot = jnp.where(down == iota((pairs, wide), 1), 1.0, 0.0).astype(BF16)
    picks[...] = jnp.concatenate([hot, hot], axis=1)
    for load in loads[1:]:
        load.wait()

    def weigh(at):
        u = frac_ref[:, at]
        g = geom_ref[:, at] * (1.0 / 6.0)
        square = u * u
        cube = square * u
        less = 1.0 - u
        gw[0, :, at] = g * (less * less * less)
        gw[1, :, at] = g * (3.0 * cube - 6.0 * square + 4.0)
        gw[2, :, at] = g * (-3.0 * cube + 3.0 * square + 3.0 * u + 1.0)
        gw[3, :, at] = g * cube

    def backward(value_of, first):
        def block(b, carry):
            values = value_of(b)
            for k in range(8):
                at = pl.ds(pl.multiple_of((8 * b + k) * LANES, LANES), LANES)
                if first:
                    weigh(at)
                knot = knot_ref[:, at]
                high, low = knot >> 4, knot & (LOW - 1)
                value = values[k:k + 1, :]
                terms = [gw[j, :, at] * value for j in range(4)]
                hits = [low == m for m in range(LOW)]
                parts = []
                for m in range(SPREAD):
                    part = jnp.zeros((nb, LANES), F32)
                    for j in range(4):
                        if 0 <= m - j < LOW:
                            part = jnp.where(hits[m - j], terms[j], part)
                    parts.append(part)
                right = jnp.concatenate(split(jnp.concatenate(parts, axis=0)), axis=1)
                left = jnp.concatenate([jnp.where(high == h, 1.0, 0.0) for h in range(HIGHS)], axis=0).astype(BF16)
                left = jnp.concatenate([left, left], axis=1)
                prod = lax.dot_general(left, right, (((1,), (1,)), ((), ())), preferred_element_type=F32)
                prod = jnp.where(same_slot, prod, 0.0)
                for h in range(HIGHS):
                    z[h, pl.ds(pl.multiple_of((8 * b + k) * nb, nb), nb), :] = prod[h * nb:(h + 1) * nb, :]
            return carry

        lax.fori_loop(0, tiles // 8, block, 0)
        if not first:
            send_norm(image_ref[...], 0)
        grad = jnp.zeros((per_coef, 2 * LANES), F32)
        for h in range(HIGHS):
            chosen = jnp.dot(picks_t[...], jnp.concatenate(split(z[h]), axis=0), preferred_element_type=F32)
            for piece in split(chosen):
                grad = grad + jnp.dot(piece, fold[h], preferred_element_type=F32)
        tail = grad[:quarter, LANES:]
        for q in range(1, 4):
            tail = tail + pltpu.roll(grad[q * quarter:(q + 1) * quarter, LANES:], 32 * q, 1)
        filled = per_coef + quarter
        return jnp.concatenate([grad[:, :LANES], tail, jnp.zeros((n * share - filled, LANES), F32)], axis=0)

    def tails(packed):
        tail = packed[per_coef:per_coef + quarter, :]
        return [tail] + [pltpu.roll(tail, LANES - 32 * q, 1) for q in range(1, 4)]

    def forward(packed, out):
        upper = jnp.concatenate(tails(packed) + [jnp.zeros((wide - per_coef, LANES), F32)], axis=0)
        lower = jnp.concatenate([packed[:per_coef, :], jnp.zeros((wide - per_coef, LANES), F32)], axis=0)
        coeffs = jnp.concatenate([lower, upper], axis=1)
        table[...] = jnp.dot(picks[...], jnp.concatenate(split(coeffs), axis=0), preferred_element_type=F32)

        def block(b, carry):
            sums = []
            for k in range(8):
                at = pl.ds(pl.multiple_of((8 * b + k) * LANES, LANES), LANES)
                span = pl.ds(pl.multiple_of((8 * b + k) * nb, nb), nb)
                below, above = table[span, :LANES], table[span, LANES:]
                knot = knot_ref[:, at]
                force = jnp.zeros((nb, LANES), F32)
                for j in range(4):
                    index = knot + j
                    lane = index & (LANES - 1)
                    found = jnp.where(
                        index < LANES,
                        jnp.take_along_axis(below, lane, axis=1, mode="promise_in_bounds"),
                        jnp.take_along_axis(above, lane, axis=1, mode="promise_in_bounds"),
                    )
                    force = force + gw[j, :, at] * found
                sums.append(jnp.sum(force, axis=0, keepdims=True))
            im_buf[out, at_coef, b] = jnp.concatenate(sums, axis=0)
            each(nc - 1, lambda k: image_copy(out, b, coef_peer(k + 1), at_coef).start())
            return carry

        lax.fori_loop(0, tiles // 8, block, 0)

    def image_copy(phase, b, p, slot):
        return pltpu.make_async_remote_copy(
            src_ref=im_buf.at[phase, slot, b], dst_ref=im_buf.at[phase, slot, b],
            send_sem=im_send.at[phase, b, p], recv_sem=im_recv.at[phase, b, slot],
            device_id=coef_id(p), device_id_type=MESH)

    def image_block(phase, b):
        def wait(k):
            p = coef_peer(k + 1)
            image_copy(phase, b, p, p).wait_recv()

        each(nc - 1, wait)
        sums = im_buf[phase, 0, b]
        for p in range(1, nc):
            sums = sums + im_buf[phase, p, b]
        return sums

    def copies(kind, phase, step, incoming=False):
        near = kind == "gm"
        p = coef_peer(step) if near else member(step)
        slot = p if incoming else (at_coef if near else me)
        target = coef_id(p) if near else member_id(p)
        if kind == "rs":
            return (send_buf.at[phase, p], rs_buf.at[phase, slot], rs_send.at[phase, p], rs_recv.at[phase, slot], target)
        buf, send, recv = dict(ag=(ag_buf, ag_send, ag_recv), gm=(gm_buf, gm_send, gm_recv), nm=(nm_buf, nm_send, nm_recv))[kind]
        return (buf.at[phase, slot], buf.at[phase, slot], send.at[phase, p], recv.at[phase, slot], target)

    def remote(parts):
        return pltpu.make_async_remote_copy(src_ref=parts[0], dst_ref=parts[1], send_sem=parts[2], recv_sem=parts[3], device_id=parts[4], device_id_type=MESH)

    def start(kind, phase, count):
        each(count - 1, lambda k: remote(copies(kind, phase, k + 1)).start())

    def arrive(kind, phase, count):
        each(count - 1, lambda k: remote(copies(kind, phase, k + 1, True)).wait_recv())

    def drain(kind, phase, count):
        each(count - 1, lambda k: remote(copies(kind, phase, k + 1)).wait_send())

    def scatter_sum(packed, phase):
        for p in range(n):
            send_buf[phase, p] = packed[p * share:(p + 1) * share, :]
        start("rs", phase, n)
        rs_buf[phase, me] = send_buf[phase, me]
        arrive("rs", phase, n)
        sums = rs_buf[phase, 0]
        for p in range(1, n):
            sums = sums + rs_buf[phase, p]
        return sums

    def gather(part, phase):
        ag_buf[phase, me] = part
        start("ag", phase, n)
        arrive("ag", phase, n)
        return ag_buf[phase].reshape(n * share, LANES)

    def send_gamma(packed, phase):
        gm_buf[phase, at_coef] = jnp.broadcast_to(total_of(packed * packed), (8, LANES))
        start("gm", phase, nc)

    def send_norm(image, phase):
        nm_buf[phase, me] = jnp.broadcast_to(total_of(image * image), (8, LANES))
        start("nm", phase, n)

    def scalar(kind, buf, phase, count):
        arrive(kind, phase, count)
        total = buf[phase, 0, :1, :1]
        for p in range(1, count):
            total = total + buf[phase, p, :1, :1]
        return total

    def target_block(b):
        return targ_ref[pl.ds(pl.multiple_of(8 * b, 8), 8), :]

    def image_values(b):
        values = image_block(0, b)
        image_ref[pl.ds(pl.multiple_of(8 * b, 8), 8), :] = values
        return values

    packed = backward(target_block, True)
    pl.semaphore_wait(barrier, n - 1 + nc - 1)
    part = scatter_sum(packed, 0)
    grad = gather(part, 0)
    send_gamma(grad, 0)
    forward(grad, 0)
    packed = backward(image_values, False)
    sums = scatter_sum(packed, 1)
    gamma = scalar("gm", gm_buf, 0, nc)
    alpha = gamma / scalar("nm", nm_buf, 0, n)
    grad_next = gather(part - alpha * sums, 1)
    send_gamma(grad_next, 1)
    forward(grad_next, 1)
    gamma_next = scalar("gm", gm_buf, 1, nc)
    beta = gamma_next / gamma
    direction = grad_next + beta * grad
    image = image_ref[...]
    image_next = jnp.concatenate([image_block(1, b) for b in range(tiles // 8)], axis=0) + beta * image
    send_norm(image_next, 1)
    alpha_next = gamma_next / scalar("nm", nm_buf, 1, n)
    answer = alpha * grad + alpha_next * direction
    sol_ref[:, :LANES] = answer[:per_coef]
    for q, tail in enumerate(tails(answer)):
        sol_ref[q * quarter:(q + 1) * quarter, LANES:] = tail[:, :NK - LANES]
    res_ref[...] = targ_ref[...] - alpha * image - alpha_next * image_next
    for phase in range(2):
        drain("rs", phase, n)
        drain("ag", phase, n)
        drain("gm", phase, nc)
        drain("nm", phase, n)
        for b in range(tiles // 8):
            each(nc - 1, lambda k: image_copy(phase, b, coef_peer(k + 1), at_coef).wait_send())


def on_device(n, nd, nc, geometry, fraction, interval, pattern, target):
    nb, rows = geometry.shape
    tiles = rows // LANES
    pairs = tiles * nb
    per_coef = TYPES // nc
    wide = -(-per_coef // LANES) * LANES
    share = -(-(per_coef + per_coef // 4) // (8 * n)) * 8
    sem = pltpu.SemaphoreType.DMA
    vmem = pl.BlockSpec(memory_space=pltpu.VMEM)
    solved, left = pl.pallas_call(
        functools.partial(kernel, n, nd, nc, share),
        out_shape=(jax.ShapeDtypeStruct((per_coef, NK), F32), jax.ShapeDtypeStruct((tiles, LANES), F32)),
        in_specs=[pl.BlockSpec(memory_space=pltpu.MemorySpace.HBM)] * 5,
        out_specs=(vmem, vmem),
        scratch_shapes=[
            pltpu.VMEM((nb, rows), F32),
            pltpu.VMEM((nb, rows), F32),
            pltpu.VMEM((nb, rows), jnp.int32),
            pltpu.VMEM((nb, tiles), jnp.int32),
            pltpu.VMEM((tiles, LANES), F32),
            pltpu.VMEM((tiles, LANES), F32),
            pltpu.VMEM((4, nb, rows), F32),
            pltpu.VMEM((HIGHS, pairs, SPREAD * nb), F32),
            pltpu.VMEM((pairs, 2 * LANES), F32),
            pltpu.VMEM((pairs, 2 * wide), BF16),
            pltpu.VMEM((per_coef, 2 * pairs), BF16),
            pltpu.VMEM((HIGHS, SPREAD * nb, 2 * LANES), BF16),
            pltpu.VMEM((2, n, share, LANES), F32),
            pltpu.VMEM((2, n, share, LANES), F32),
            pltpu.VMEM((2, n, share, LANES), F32),
            pltpu.VMEM((2, nc, tiles // 8, 8, LANES), F32),
            pltpu.VMEM((2, nc, 8, LANES), F32),
            pltpu.VMEM((2, n, 8, LANES), F32),
            sem((5,)),
            sem((2, n)), sem((2, n)), sem((2, n)), sem((2, n)),
            sem((2, tiles // 8, nc)), sem((2, tiles // 8, nc)),
            sem((2, nc)), sem((2, nc)), sem((2, n)), sem((2, n)),
        ],
        compiler_params=pltpu.CompilerParams(collective_id=0, has_side_effects=True, vmem_limit_bytes=63 * 1024 * 1024),
    )(geometry, fraction, interval, pattern, target.reshape(tiles, LANES))
    return solved, left.reshape(rows)


def solution(mesh):
    sizes = dict(mesh.shape)
    n, nd, nc = sizes["frame"] * sizes["dom"], sizes["dom"], sizes["coef"]
    both = P("coef", ("frame", "dom"))
    return jax.shard_map(
        functools.partial(on_device, n, nd, nc),
        mesh=mesh,
        in_specs=(both, both, both, both, P(("frame", "dom"))),
        out_specs=(P("coef", None), P(("frame", "dom"))),
        check_vma=False,
    )
```

```python
import functools

import jax
import jax.numpy as jnp
from jax import lax
from jax.experimental import pallas as pl
from jax.experimental.pallas import tpu as pltpu
from jax.sharding import PartitionSpec as P

NK = 160
TYPES = 384
LANES = 128
LOW = 13
HIGHS = -(-(NK - 3) // LOW)
SPREAD = LOW + 3
MESH = pl.DeviceIdType.MESH
F32 = jnp.float32
BF16 = jnp.bfloat16


def iota(shape, axis):
    return lax.broadcasted_iota(jnp.int32, shape, axis)


def split(x):
    top = x.astype(BF16)
    return top, (x - top.astype(F32)).astype(BF16)


def total_of(x):
    return jnp.sum(jnp.sum(x, axis=0, keepdims=True), axis=1, keepdims=True)


def each(count, body):
    if count <= 8:
        for index in range(count):
            body(index)
    else:
        lax.fori_loop(0, count, lambda index, _: (body(index), 0)[1], 0)


def kernel(n, nd, nc, share, geom_hbm, frac_hbm, knot_hbm, patt_hbm, targ_hbm, sol_ref, res_ref,
           geom_ref, frac_ref, knot_ref, patt_ref, targ_ref, image_ref,
           gw, z, table, picks, picks_t, fold, send_buf, rs_buf, ag_buf, im_buf, gm_buf, nm_buf, load_sem,
           rs_send, rs_recv, ag_send, ag_recv, im_send, im_recv, gm_send, gm_recv, nm_send, nm_recv):
    loads = [
        pltpu.make_async_copy(src, dst, load_sem.at[k])
        for k, (src, dst) in enumerate(((patt_hbm, patt_ref), (frac_hbm, frac_ref), (geom_hbm, geom_ref), (knot_hbm, knot_ref), (targ_hbm, targ_ref)))
    ]
    for load in loads:
        load.start()
    nb, rows = geom_ref.shape
    tiles = rows // LANES
    pairs = tiles * nb
    per_coef = TYPES // nc
    wide = picks.shape[1] // 2
    quarter = per_coef // 4
    at_dom = lax.axis_index("dom")
    at_coef = lax.axis_index("coef")
    at_frame = lax.axis_index("frame")
    me = at_frame * nd + at_dom

    def member(step):
        return lax.rem(me + step, n)

    def member_id(p):
        return (lax.div(p, nd), lax.rem(p, nd), at_coef)

    def coef_peer(step):
        return lax.rem(at_coef + step, nc)

    def coef_id(p):
        return (at_frame, at_dom, p)

    barrier = pltpu.get_barrier_semaphore()
    each(n - 1, lambda k: pl.semaphore_signal(barrier, inc=1, device_id=member_id(member(k + 1)), device_id_type=MESH))
    each(nc - 1, lambda k: pl.semaphore_signal(barrier, inc=1, device_id=coef_id(coef_peer(k + 1)), device_id_type=MESH))

    inner = SPREAD * nb
    lows = iota((inner, 2 * LANES), 0) // nb
    for h in range(HIGHS):
        hot = jnp.where(iota((inner, 2 * LANES), 1) == lows + LOW * h, 1.0, 0.0).astype(BF16)
        fold[2 * h * inner:(2 * h + 1) * inner, :] = hot
        fold[(2 * h + 1) * inner:(2 * h + 2) * inner, :] = hot
    same_slot = (iota((nb, inner), 1) & (nb - 1)) == iota((nb, inner), 0)

    loads[0].wait()
    kinds = patt_ref[...].astype(F32).astype(BF16)
    spread = (iota((tiles, pairs), 1) >= nb * iota((tiles, pairs), 0)) & (iota((tiles, pairs), 1) < nb * (iota((tiles, pairs), 0) + 1))
    across = jnp.dot(kinds, jnp.where(spread, 1.0, 0.0).astype(BF16), preferred_element_type=F32)
    own = (iota((nb, pairs), 1) & (nb - 1)) == iota((nb, pairs), 0)
    across = jnp.sum(jnp.where(own, across, 0.0), axis=0, keepdims=True).astype(jnp.int32)
    hot_t = jnp.where(across == iota((per_coef, pairs), 0), 1.0, 0.0).astype(BF16)
    picks_t[...] = jnp.concatenate([hot_t, hot_t], axis=1)
    spread = (iota((pairs, tiles), 0) >= nb * iota((pairs, tiles), 1)) & (iota((pairs, tiles), 0) < nb * (iota((pairs, tiles), 1) + 1))
    down = lax.dot_general(jnp.where(spread, 1.0, 0.0).astype(BF16), kinds, (((1,), (1,)), ((), ())), preferred_element_type=F32)
    own = (iota((pairs, nb), 0) & (nb - 1)) == iota((pairs, nb), 1)
    down = jnp.sum(jnp.where(own, down, 0.0), axis=1, keepdims=True).astype(jnp.int32)
    hot = jnp.where(down == iota((pairs, wide), 1), 1.0, 0.0).astype(BF16)
    picks[...] = jnp.concatenate([hot, hot], axis=1)
    for load in loads[1:]:
        load.wait()

    def weigh(at):
        u = frac_ref[:, at]
        g = geom_ref[:, at] * (1.0 / 6.0)
        square = u * u
        cube = square * u
        less = 1.0 - u
        gw[0, :, at] = g * (less * less * less)
        gw[1, :, at] = g * (3.0 * cube - 6.0 * square + 4.0)
        gw[2, :, at] = g * (-3.0 * cube + 3.0 * square + 3.0 * u + 1.0)
        gw[3, :, at] = g * cube

    def backward(value_of, first):
        def block(b, carry):
            values = value_of(b)
            def product(k):
                at = pl.ds(pl.multiple_of((8 * b + k) * LANES, LANES), LANES)
                if first:
                    weigh(at)
                knot = knot_ref[:, at]
                high = (knot * 79) >> 10
                low = knot - LOW * high
                value = values[k:k + 1, :]
                terms = [gw[j, :, at] * value for j in range(4)]
                hits = [low == m for m in range(LOW)]
                parts = []
                for m in range(SPREAD):
                    part = jnp.zeros((nb, LANES), F32)
                    for j in range(4):
                        if 0 <= m - j < LOW:
                            part = jnp.where(hits[m - j], terms[j], part)
                    parts.append(part)
                right = jnp.concatenate(split(jnp.concatenate(parts, axis=0)), axis=1)
                left = [jnp.where(high == h, 1.0, 0.0) for h in range(HIGHS)]
                left = jnp.concatenate(left + [jnp.zeros((nb, LANES), F32)] * (HIGHS % 2), axis=0).astype(BF16)
                left = jnp.concatenate([left, left], axis=1)
                prod = lax.dot_general(left, right, (((1,), (1,)), ((), ())), preferred_element_type=F32)
                return [jnp.where(same_slot, prod[h * nb:(h + 1) * nb, :], 0.0) for h in range(HIGHS)]

            for k in range(0, 8, 2):
                span = pl.ds(pl.multiple_of((8 * b + k) * nb, 2 * nb), 2 * nb)
                for h, two in enumerate(zip(product(k), product(k + 1))):
                    top, rest = split(jnp.concatenate(two, axis=0))
                    z[span, 2 * h * inner:(2 * h + 1) * inner] = top
                    z[span, (2 * h + 1) * inner:(2 * h + 2) * inner] = rest
            return carry

        lax.fori_loop(0, tiles // 8, block, 0)
        if not first:
            send_norm(image_ref[...], 0)
        folded = jnp.dot(z[...], fold[...], preferred_element_type=F32)
        grad = jnp.dot(picks_t[...], jnp.concatenate(split(folded), axis=0), preferred_element_type=F32)
        tail = grad[:quarter, LANES:]
        for q in range(1, 4):
            tail = tail + pltpu.roll(grad[q * quarter:(q + 1) * quarter, LANES:], 32 * q, 1)
        filled = per_coef + quarter
        return jnp.concatenate([grad[:, :LANES], tail, jnp.zeros((n * share - filled, LANES), F32)], axis=0)

    def tails(packed):
        tail = packed[per_coef:per_coef + quarter, :]
        return [tail] + [pltpu.roll(tail, LANES - 32 * q, 1) for q in range(1, 4)]

    def forward(packed, out):
        upper = jnp.concatenate(tails(packed) + [jnp.zeros((wide - per_coef, LANES), F32)], axis=0)
        lower = jnp.concatenate([packed[:per_coef, :], jnp.zeros((wide - per_coef, LANES), F32)], axis=0)
        coeffs = jnp.concatenate([lower, upper], axis=1)
        table[...] = jnp.dot(picks[...], jnp.concatenate(split(coeffs), axis=0), preferred_element_type=F32)

        def block(b, carry):
            sums = []
            for k in range(8):
                at = pl.ds(pl.multiple_of((8 * b + k) * LANES, LANES), LANES)
                span = pl.ds(pl.multiple_of((8 * b + k) * nb, nb), nb)
                below, above = table[span, :LANES], table[span, LANES:]
                knot = knot_ref[:, at]
                force = jnp.zeros((nb, LANES), F32)
                for j in range(4):
                    index = knot + j
                    lane = index & (LANES - 1)
                    found = jnp.where(
                        index < LANES,
                        jnp.take_along_axis(below, lane, axis=1, mode="promise_in_bounds"),
                        jnp.take_along_axis(above, lane, axis=1, mode="promise_in_bounds"),
                    )
                    force = force + gw[j, :, at] * found
                sums.append(jnp.sum(force, axis=0, keepdims=True))
            im_buf[out, at_coef, b] = jnp.concatenate(sums, axis=0)
            each(nc - 1, lambda k: image_copy(out, b, coef_peer(k + 1), at_coef).start())
            return carry

        lax.fori_loop(0, tiles // 8, block, 0)

    def image_copy(phase, b, p, slot):
        return pltpu.make_async_remote_copy(
            src_ref=im_buf.at[phase, slot, b], dst_ref=im_buf.at[phase, slot, b],
            send_sem=im_send.at[phase, b, p], recv_sem=im_recv.at[phase, b, slot],
            device_id=coef_id(p), device_id_type=MESH)

    def image_block(phase, b):
        def wait(k):
            p = coef_peer(k + 1)
            image_copy(phase, b, p, p).wait_recv()

        each(nc - 1, wait)
        sums = im_buf[phase, 0, b]
        for p in range(1, nc):
            sums = sums + im_buf[phase, p, b]
        return sums

    def copies(kind, phase, step, incoming=False):
        near = kind == "gm"
        p = coef_peer(step) if near else member(step)
        slot = p if incoming else (at_coef if near else me)
        target = coef_id(p) if near else member_id(p)
        if kind == "rs":
            return (send_buf.at[phase, p], rs_buf.at[phase, slot], rs_send.at[phase, p], rs_recv.at[phase, slot], target)
        buf, send, recv = dict(ag=(ag_buf, ag_send, ag_recv), gm=(gm_buf, gm_send, gm_recv), nm=(nm_buf, nm_send, nm_recv))[kind]
        return (buf.at[phase, slot], buf.at[phase, slot], send.at[phase, p], recv.at[phase, slot], target)

    def remote(parts):
        return pltpu.make_async_remote_copy(src_ref=parts[0], dst_ref=parts[1], send_sem=parts[2], recv_sem=parts[3], device_id=parts[4], device_id_type=MESH)

    def start(kind, phase, count):
        each(count - 1, lambda k: remote(copies(kind, phase, k + 1)).start())

    def arrive(kind, phase, count):
        each(count - 1, lambda k: remote(copies(kind, phase, k + 1, True)).wait_recv())

    def drain(kind, phase, count):
        each(count - 1, lambda k: remote(copies(kind, phase, k + 1)).wait_send())

    def scatter_sum(packed, phase):
        for p in range(n):
            send_buf[phase, p] = packed[p * share:(p + 1) * share, :]
        start("rs", phase, n)
        rs_buf[phase, me] = send_buf[phase, me]
        arrive("rs", phase, n)
        sums = rs_buf[phase, 0]
        for p in range(1, n):
            sums = sums + rs_buf[phase, p]
        return sums

    def gather(part, phase):
        ag_buf[phase, me] = part
        start("ag", phase, n)
        arrive("ag", phase, n)
        return ag_buf[phase].reshape(n * share, LANES)

    def send_gamma(packed, phase):
        gm_buf[phase, at_coef] = jnp.broadcast_to(total_of(packed * packed), (8, LANES))
        start("gm", phase, nc)

    def send_norm(image, phase):
        nm_buf[phase, me] = jnp.broadcast_to(total_of(image * image), (8, LANES))
        start("nm", phase, n)

    def scalar(kind, buf, phase, count):
        arrive(kind, phase, count)
        total = buf[phase, 0, :1, :1]
        for p in range(1, count):
            total = total + buf[phase, p, :1, :1]
        return total

    def target_block(b):
        return targ_ref[pl.ds(pl.multiple_of(8 * b, 8), 8), :]

    def image_values(b):
        values = image_block(0, b)
        image_ref[pl.ds(pl.multiple_of(8 * b, 8), 8), :] = values
        return values

    packed = backward(target_block, True)
    pl.semaphore_wait(barrier, n - 1 + nc - 1)
    part = scatter_sum(packed, 0)
    grad = gather(part, 0)
    send_gamma(grad, 0)
    forward(grad, 0)
    packed = backward(image_values, False)
    sums = scatter_sum(packed, 1)
    gamma = scalar("gm", gm_buf, 0, nc)
    alpha = gamma / scalar("nm", nm_buf, 0, n)
    grad_next = gather(part - alpha * sums, 1)
    send_gamma(grad_next, 1)
    forward(grad_next, 1)
    gamma_next = scalar("gm", gm_buf, 1, nc)
    beta = gamma_next / gamma
    direction = grad_next + beta * grad
    image = image_ref[...]
    image_next = jnp.concatenate([image_block(1, b) for b in range(tiles // 8)], axis=0) + beta * image
    send_norm(image_next, 1)
    alpha_next = gamma_next / scalar("nm", nm_buf, 1, n)
    answer = alpha * grad + alpha_next * direction
    tail = jnp.concatenate(tails(answer), axis=0)
    sol_ref[:LANES, :] = answer[:per_coef].T
    sol_ref[LANES:, :] = tail.T[:NK - LANES, :]
    res_ref[...] = targ_ref[...] - alpha * image - alpha_next * image_next
    for phase in range(2):
        drain("rs", phase, n)
        drain("ag", phase, n)
        drain("gm", phase, nc)
        drain("nm", phase, n)
        for b in range(tiles // 8):
            each(nc - 1, lambda k: image_copy(phase, b, coef_peer(k + 1), at_coef).wait_send())


def on_device(n, nd, nc, geometry, fraction, interval, pattern, target):
    nb, rows = geometry.shape
    tiles = rows // LANES
    pairs = tiles * nb
    per_coef = TYPES // nc
    wide = -(-per_coef // LANES) * LANES
    share = -(-(per_coef + per_coef // 4) // (8 * n)) * 8
    sem = pltpu.SemaphoreType.DMA
    vmem = pl.BlockSpec(memory_space=pltpu.VMEM)
    solved, left = pl.pallas_call(
        functools.partial(kernel, n, nd, nc, share),
        out_shape=(jax.ShapeDtypeStruct((NK, per_coef), F32), jax.ShapeDtypeStruct((tiles, LANES), F32)),
        in_specs=[pl.BlockSpec(memory_space=pltpu.MemorySpace.HBM)] * 5,
        out_specs=(vmem, vmem),
        scratch_shapes=[
            pltpu.VMEM((nb, rows), F32),
            pltpu.VMEM((nb, rows), F32),
            pltpu.VMEM((nb, rows), jnp.int32),
            pltpu.VMEM((nb, tiles), jnp.int32),
            pltpu.VMEM((tiles, LANES), F32),
            pltpu.VMEM((tiles, LANES), F32),
            pltpu.VMEM((4, nb, rows), F32),
            pltpu.VMEM((pairs, 2 * HIGHS * SPREAD * nb), BF16),
            pltpu.VMEM((pairs, 2 * LANES), F32),
            pltpu.VMEM((pairs, 2 * wide), BF16),
            pltpu.VMEM((per_coef, 2 * pairs), BF16),
            pltpu.VMEM((2 * HIGHS * SPREAD * nb, 2 * LANES), BF16),
            pltpu.VMEM((2, n, share, LANES), F32),
            pltpu.VMEM((2, n, share, LANES), F32),
            pltpu.VMEM((2, n, share, LANES), F32),
            pltpu.VMEM((2, nc, tiles // 8, 8, LANES), F32),
            pltpu.VMEM((2, nc, 8, LANES), F32),
            pltpu.VMEM((2, n, 8, LANES), F32),
            sem((5,)),
            sem((2, n)), sem((2, n)), sem((2, n)), sem((2, n)),
            sem((2, tiles // 8, nc)), sem((2, tiles // 8, nc)),
            sem((2, nc)), sem((2, nc)), sem((2, n)), sem((2, n)),
        ],
        compiler_params=pltpu.CompilerParams(collective_id=0, has_side_effects=True, vmem_limit_bytes=63 * 1024 * 1024),
    )(geometry, fraction, interval, pattern, target.reshape(tiles, LANES))
    return solved.T, left.reshape(rows)


def solution(mesh):
    sizes = dict(mesh.shape)
    n, nd, nc = sizes["frame"] * sizes["dom"], sizes["dom"], sizes["coef"]
    both = P("coef", ("frame", "dom"))
    return jax.shard_map(
        functools.partial(on_device, n, nd, nc),
        mesh=mesh,
        in_specs=(both, both, both, both, P(("frame", "dom"))),
        out_specs=(P("coef", None), P(("frame", "dom"))),
        check_vma=False,
    )
```

```python
import functools

import jax
import jax.numpy as jnp
from jax import lax
from jax.experimental import pallas as pl
from jax.experimental.pallas import tpu as pltpu
from jax.sharding import PartitionSpec as P

NK = 160
TYPES = 384
LANES = 128
LOW = 13
HIGHS = -(-(NK - 3) // LOW)
SPREAD = LOW + 3
MESH = pl.DeviceIdType.MESH
F32 = jnp.float32
BF16 = jnp.bfloat16


def iota(shape, axis):
    return lax.broadcasted_iota(jnp.int32, shape, axis)


def split(x):
    top = x.astype(BF16)
    return top, (x - top.astype(F32)).astype(BF16)


def total_of(x):
    return jnp.sum(jnp.sum(x, axis=0, keepdims=True), axis=1, keepdims=True)


def each(count, body):
    if count <= 8:
        for index in range(count):
            body(index)
    else:
        lax.fori_loop(0, count, lambda index, _: (body(index), 0)[1], 0)


def kernel(nf, nd, nc, share, geom_hbm, frac_hbm, knot_hbm, patt_hbm, targ_hbm, sol_ref, res_ref,
           geom_ref, frac_ref, knot_ref, patt_ref, targ_ref, image_ref,
           gw, z, table, picks, picks_t, fold, send_buf, rs_buf, fr_buf, ag_buf, im_buf, gm_buf, nm_buf, load_sem,
           rs_send, rs_recv, fr_send, fr_recv, ag_send, ag_recv, im_send, im_recv, gm_send, gm_recv, nm_send, nm_recv):
    loads = [
        pltpu.make_async_copy(src, dst, load_sem.at[k])
        for k, (src, dst) in enumerate(((patt_hbm, patt_ref), (frac_hbm, frac_ref), (geom_hbm, geom_ref), (knot_hbm, knot_ref), (targ_hbm, targ_ref)))
    ]
    for load in loads:
        load.start()
    nb, rows = geom_ref.shape
    tiles = rows // LANES
    pairs = tiles * nb
    per_coef = TYPES // nc
    wide = picks.shape[1] // 2
    quarter = per_coef // 4
    at_dom = lax.axis_index("dom")
    at_coef = lax.axis_index("coef")
    at_frame = lax.axis_index("frame")
    me = at_frame * nd + at_dom
    n = nf * nd

    def member(step):
        return lax.rem(me + step, n)

    def member_id(p):
        return (lax.div(p, nd), lax.rem(p, nd), at_coef)

    def coef_peer(step):
        return lax.rem(at_coef + step, nc)

    def coef_id(p):
        return (at_frame, at_dom, p)

    def dom_peer(step):
        return lax.rem(at_dom + step, nd)

    def frame_peer(step):
        return lax.rem(at_frame + step, nf)

    barrier = pltpu.get_barrier_semaphore()
    each(n - 1, lambda k: pl.semaphore_signal(barrier, inc=1, device_id=member_id(member(k + 1)), device_id_type=MESH))
    each(nc - 1, lambda k: pl.semaphore_signal(barrier, inc=1, device_id=coef_id(coef_peer(k + 1)), device_id_type=MESH))

    inner = SPREAD * nb
    lows = iota((inner, 2 * LANES), 0) // nb
    for h in range(HIGHS):
        hot = jnp.where(iota((inner, 2 * LANES), 1) == lows + LOW * h, 1.0, 0.0).astype(BF16)
        fold[2 * h * inner:(2 * h + 1) * inner, :] = hot
        fold[(2 * h + 1) * inner:(2 * h + 2) * inner, :] = hot
    same_slot = (iota((nb, inner), 1) & (nb - 1)) == iota((nb, inner), 0)

    loads[0].wait()
    kinds = patt_ref[...].astype(F32).astype(BF16)
    spread = (iota((tiles, pairs), 1) >= nb * iota((tiles, pairs), 0)) & (iota((tiles, pairs), 1) < nb * (iota((tiles, pairs), 0) + 1))
    across = jnp.dot(kinds, jnp.where(spread, 1.0, 0.0).astype(BF16), preferred_element_type=F32)
    own = (iota((nb, pairs), 1) & (nb - 1)) == iota((nb, pairs), 0)
    across = jnp.sum(jnp.where(own, across, 0.0), axis=0, keepdims=True).astype(jnp.int32)
    hot_t = jnp.where(across == iota((per_coef, pairs), 0), 1.0, 0.0).astype(BF16)
    picks_t[...] = jnp.concatenate([hot_t, hot_t], axis=1)
    spread = (iota((pairs, tiles), 0) >= nb * iota((pairs, tiles), 1)) & (iota((pairs, tiles), 0) < nb * (iota((pairs, tiles), 1) + 1))
    down = lax.dot_general(jnp.where(spread, 1.0, 0.0).astype(BF16), kinds, (((1,), (1,)), ((), ())), preferred_element_type=F32)
    own = (iota((pairs, nb), 0) & (nb - 1)) == iota((pairs, nb), 1)
    down = jnp.sum(jnp.where(own, down, 0.0), axis=1, keepdims=True).astype(jnp.int32)
    hot = jnp.where(down == iota((pairs, wide), 1), 1.0, 0.0).astype(BF16)
    picks[...] = jnp.concatenate([hot, hot], axis=1)
    for load in loads[1:]:
        load.wait()

    def weigh(at):
        u = frac_ref[:, at]
        g = geom_ref[:, at] * (1.0 / 6.0)
        square = u * u
        cube = square * u
        less = 1.0 - u
        gw[0, :, at] = g * (less * less * less)
        gw[1, :, at] = g * (3.0 * cube - 6.0 * square + 4.0)
        gw[2, :, at] = g * (-3.0 * cube + 3.0 * square + 3.0 * u + 1.0)
        gw[3, :, at] = g * cube

    def backward(value_of, first):
        def block(b, carry):
            values = value_of(b)
            def product(k):
                at = pl.ds(pl.multiple_of((8 * b + k) * LANES, LANES), LANES)
                if first:
                    weigh(at)
                knot = knot_ref[:, at]
                high = (knot * 79) >> 10
                low = knot - LOW * high
                value = values[k:k + 1, :]
                terms = [gw[j, :, at] * value for j in range(4)]
                hits = [low == m for m in range(LOW)]
                parts = []
                for m in range(SPREAD):
                    part = jnp.zeros((nb, LANES), F32)
                    for j in range(4):
                        if 0 <= m - j < LOW:
                            part = jnp.where(hits[m - j], terms[j], part)
                    parts.append(part)
                right = jnp.concatenate(split(jnp.concatenate(parts, axis=0)), axis=1)
                left = [jnp.where(high == h, 1.0, 0.0) for h in range(HIGHS)]
                left = jnp.concatenate(left + [jnp.zeros((nb, LANES), F32)] * (HIGHS % 2), axis=0).astype(BF16)
                left = jnp.concatenate([left, left], axis=1)
                prod = lax.dot_general(left, right, (((1,), (1,)), ((), ())), preferred_element_type=F32)
                return [jnp.where(same_slot, prod[h * nb:(h + 1) * nb, :], 0.0) for h in range(HIGHS)]

            for k in range(0, 8, 2):
                span = pl.ds(pl.multiple_of((8 * b + k) * nb, 2 * nb), 2 * nb)
                for h, two in enumerate(zip(product(k), product(k + 1))):
                    top, rest = split(jnp.concatenate(two, axis=0))
                    z[span, 2 * h * inner:(2 * h + 1) * inner] = top
                    z[span, (2 * h + 1) * inner:(2 * h + 2) * inner] = rest
            return carry

        lax.fori_loop(0, tiles // 8, block, 0)
        if not first:
            send_norm(image_ref[...], 0)
        folded = jnp.dot(z[...], fold[...], preferred_element_type=F32)
        grad = jnp.dot(picks_t[...], jnp.concatenate(split(folded), axis=0), preferred_element_type=F32)
        tail = grad[:quarter, LANES:]
        for q in range(1, 4):
            tail = tail + pltpu.roll(grad[q * quarter:(q + 1) * quarter, LANES:], 32 * q, 1)
        filled = per_coef + quarter
        return jnp.concatenate([grad[:, :LANES], tail, jnp.zeros((nd * share - filled, LANES), F32)], axis=0)

    def tails(packed):
        tail = packed[per_coef:per_coef + quarter, :]
        return [tail] + [pltpu.roll(tail, LANES - 32 * q, 1) for q in range(1, 4)]

    def forward(packed, out):
        upper = jnp.concatenate(tails(packed) + [jnp.zeros((wide - per_coef, LANES), F32)], axis=0)
        lower = jnp.concatenate([packed[:per_coef, :], jnp.zeros((wide - per_coef, LANES), F32)], axis=0)
        coeffs = jnp.concatenate([lower, upper], axis=1)
        table[...] = jnp.dot(picks[...], jnp.concatenate(split(coeffs), axis=0), preferred_element_type=F32)

        def block(b, carry):
            sums = []
            for k in range(8):
                at = pl.ds(pl.multiple_of((8 * b + k) * LANES, LANES), LANES)
                span = pl.ds(pl.multiple_of((8 * b + k) * nb, nb), nb)
                below, above = table[span, :LANES], table[span, LANES:]
                knot = knot_ref[:, at]
                force = jnp.zeros((nb, LANES), F32)
                for j in range(4):
                    index = knot + j
                    lane = index & (LANES - 1)
                    found = jnp.where(
                        index < LANES,
                        jnp.take_along_axis(below, lane, axis=1, mode="promise_in_bounds"),
                        jnp.take_along_axis(above, lane, axis=1, mode="promise_in_bounds"),
                    )
                    force = force + gw[j, :, at] * found
                sums.append(jnp.sum(force, axis=0, keepdims=True))
            im_buf[out, at_coef, b] = jnp.concatenate(sums, axis=0)
            each(nc - 1, lambda k: image_copy(out, b, coef_peer(k + 1), at_coef).start())
            return carry

        lax.fori_loop(0, tiles // 8, block, 0)

    def image_copy(phase, b, p, slot):
        return pltpu.make_async_remote_copy(
            src_ref=im_buf.at[phase, slot, b], dst_ref=im_buf.at[phase, slot, b],
            send_sem=im_send.at[phase, b, p], recv_sem=im_recv.at[phase, b, slot],
            device_id=coef_id(p), device_id_type=MESH)

    def image_block(phase, b):
        def wait(k):
            p = coef_peer(k + 1)
            image_copy(phase, b, p, p).wait_recv()

        each(nc - 1, wait)
        sums = im_buf[phase, 0, b]
        for p in range(1, nc):
            sums = sums + im_buf[phase, p, b]
        return sums

    def copies(kind, phase, step, incoming=False):
        p, mine, target = {
            "rs": lambda: (dom_peer(step), at_dom, lambda q: (at_frame, q, at_coef)),
            "fr": lambda: (frame_peer(step), at_frame, lambda q: (q, at_dom, at_coef)),
            "ag": lambda: (dom_peer(step), at_dom, lambda q: (at_frame, q, at_coef)),
            "gm": lambda: (coef_peer(step), at_coef, coef_id),
            "nm": lambda: (member(step), me, member_id),
        }[kind]()
        slot = p if incoming else mine
        if kind == "rs":
            return (send_buf.at[phase, p], rs_buf.at[phase, slot], rs_send.at[phase, p], rs_recv.at[phase, slot], target(p))
        buf, send, recv = dict(
            fr=(fr_buf, fr_send, fr_recv), ag=(ag_buf, ag_send, ag_recv),
            gm=(gm_buf, gm_send, gm_recv), nm=(nm_buf, nm_send, nm_recv))[kind]
        return (buf.at[phase, slot], buf.at[phase, slot], send.at[phase, p], recv.at[phase, slot], target(p))

    def remote(parts):
        return pltpu.make_async_remote_copy(src_ref=parts[0], dst_ref=parts[1], send_sem=parts[2], recv_sem=parts[3], device_id=parts[4], device_id_type=MESH)

    def start(kind, phase, count):
        each(count - 1, lambda k: remote(copies(kind, phase, k + 1)).start())

    def arrive(kind, phase, count):
        each(count - 1, lambda k: remote(copies(kind, phase, k + 1, True)).wait_recv())

    def drain(kind, phase, count):
        each(count - 1, lambda k: remote(copies(kind, phase, k + 1)).wait_send())

    def scatter_sum(packed, phase):
        for p in range(nd):
            send_buf[phase, p] = packed[p * share:(p + 1) * share, :]
        start("rs", phase, nd)
        rs_buf[phase, at_dom] = send_buf[phase, at_dom]
        arrive("rs", phase, nd)
        sums = rs_buf[phase, 0]
        for p in range(1, nd):
            sums = sums + rs_buf[phase, p]
        fr_buf[phase, at_frame] = sums
        start("fr", phase, nf)
        arrive("fr", phase, nf)
        sums = fr_buf[phase, 0]
        for p in range(1, nf):
            sums = sums + fr_buf[phase, p]
        return sums

    def gather(part, phase):
        ag_buf[phase, at_dom] = part
        start("ag", phase, nd)
        arrive("ag", phase, nd)
        return ag_buf[phase].reshape(nd * share, LANES)

    def send_gamma(packed, phase):
        gm_buf[phase, at_coef] = jnp.broadcast_to(total_of(packed * packed), (8, LANES))
        start("gm", phase, nc)

    def send_norm(image, phase):
        nm_buf[phase, me] = jnp.broadcast_to(total_of(image * image), (8, LANES))
        start("nm", phase, n)

    def scalar(kind, buf, phase, count):
        arrive(kind, phase, count)
        total = buf[phase, 0, :1, :1]
        for p in range(1, count):
            total = total + buf[phase, p, :1, :1]
        return total

    def target_block(b):
        return targ_ref[pl.ds(pl.multiple_of(8 * b, 8), 8), :]

    def image_values(b):
        values = image_block(0, b)
        image_ref[pl.ds(pl.multiple_of(8 * b, 8), 8), :] = values
        return values

    packed = backward(target_block, True)
    pl.semaphore_wait(barrier, n - 1 + nc - 1)
    part = scatter_sum(packed, 0)
    grad = gather(part, 0)
    send_gamma(grad, 0)
    forward(grad, 0)
    packed = backward(image_values, False)
    sums = scatter_sum(packed, 1)
    gamma = scalar("gm", gm_buf, 0, nc)
    alpha = gamma / scalar("nm", nm_buf, 0, n)
    grad_next = gather(part - alpha * sums, 1)
    send_gamma(grad_next, 1)
    forward(grad_next, 1)
    gamma_next = scalar("gm", gm_buf, 1, nc)
    beta = gamma_next / gamma
    direction = grad_next + beta * grad
    image = image_ref[...]
    image_next = jnp.concatenate([image_block(1, b) for b in range(tiles // 8)], axis=0) + beta * image
    send_norm(image_next, 1)
    alpha_next = gamma_next / scalar("nm", nm_buf, 1, n)
    answer = alpha * grad + alpha_next * direction
    tail = jnp.concatenate(tails(answer), axis=0)
    sol_ref[:LANES, :] = answer[:per_coef].T
    sol_ref[LANES:, :] = tail.T[:NK - LANES, :]
    res_ref[...] = targ_ref[...] - alpha * image - alpha_next * image_next
    for phase in range(2):
        drain("rs", phase, nd)
        drain("fr", phase, nf)
        drain("ag", phase, nd)
        drain("gm", phase, nc)
        drain("nm", phase, n)
        for b in range(tiles // 8):
            each(nc - 1, lambda k: image_copy(phase, b, coef_peer(k + 1), at_coef).wait_send())


def on_device(nf, nd, nc, geometry, fraction, interval, pattern, target):
    nb, rows = geometry.shape
    tiles = rows // LANES
    pairs = tiles * nb
    per_coef = TYPES // nc
    wide = -(-per_coef // LANES) * LANES
    n = nf * nd
    share = -(-(per_coef + per_coef // 4) // (8 * nd)) * 8
    sem = pltpu.SemaphoreType.DMA
    vmem = pl.BlockSpec(memory_space=pltpu.VMEM)
    solved, left = pl.pallas_call(
        functools.partial(kernel, nf, nd, nc, share),
        out_shape=(jax.ShapeDtypeStruct((NK, per_coef), F32), jax.ShapeDtypeStruct((tiles, LANES), F32)),
        in_specs=[pl.BlockSpec(memory_space=pltpu.MemorySpace.HBM)] * 5,
        out_specs=(vmem, vmem),
        scratch_shapes=[
            pltpu.VMEM((nb, rows), F32),
            pltpu.VMEM((nb, rows), F32),
            pltpu.VMEM((nb, rows), jnp.int32),
            pltpu.VMEM((nb, tiles), jnp.int32),
            pltpu.VMEM((tiles, LANES), F32),
            pltpu.VMEM((tiles, LANES), F32),
            pltpu.VMEM((4, nb, rows), F32),
            pltpu.VMEM((pairs, 2 * HIGHS * SPREAD * nb), BF16),
            pltpu.VMEM((pairs, 2 * LANES), F32),
            pltpu.VMEM((pairs, 2 * wide), BF16),
            pltpu.VMEM((per_coef, 2 * pairs), BF16),
            pltpu.VMEM((2 * HIGHS * SPREAD * nb, 2 * LANES), BF16),
            pltpu.VMEM((2, nd, share, LANES), F32),
            pltpu.VMEM((2, nd, share, LANES), F32),
            pltpu.VMEM((2, nf, share, LANES), F32),
            pltpu.VMEM((2, nd, share, LANES), F32),
            pltpu.VMEM((2, nc, tiles // 8, 8, LANES), F32),
            pltpu.VMEM((2, nc, 8, LANES), F32),
            pltpu.VMEM((2, n, 8, LANES), F32),
            sem((5,)),
            sem((2, nd)), sem((2, nd)), sem((2, nf)), sem((2, nf)), sem((2, nd)), sem((2, nd)),
            sem((2, tiles // 8, nc)), sem((2, tiles // 8, nc)),
            sem((2, nc)), sem((2, nc)), sem((2, n)), sem((2, n)),
        ],
        compiler_params=pltpu.CompilerParams(collective_id=0, has_side_effects=True, vmem_limit_bytes=63 * 1024 * 1024),
    )(geometry, fraction, interval, pattern, target.reshape(tiles, LANES))
    return solved.T, left.reshape(rows)


def solution(mesh):
    sizes = dict(mesh.shape)
    nf, nd, nc = sizes["frame"], sizes["dom"], sizes["coef"]
    both = P("coef", ("frame", "dom"))
    return jax.shard_map(
        functools.partial(on_device, nf, nd, nc),
        mesh=mesh,
        in_specs=(both, both, both, both, P(("frame", "dom"))),
        out_specs=(P("coef", None), P(("frame", "dom"))),
        check_vma=False,
    )
```
